32 devices in a mesh: aux: 16 (over z, y, x), bas: 2 (over core).
Axes of the slice: x: 2, y: 2, z: 4, core: 2. Of those that a mesh axis runs over, the one named last changes fastest.
Arguments:
- integrals: bfloat16 [16, 32, 3, 128, 128], P('aux', 'bas'), may hold values from -0.125 to 0.125
- orbitals: bfloat16 [32, 128, 128], P('bas'), may hold values from -0.5 to 0.5
- locality: int32 [32], P('bas'), may hold values from 0 to 15, as said below
- screen: int32 [16, 32, 3], P('aux', 'bas'), may hold values 0 or 1
- metric: bfloat16 [16, 16], replicated, may hold values from -1 to 3
Outputs:
- exchange_band: float32 [32, 5, 16384], P('bas', None, 'aux')
The draws below stay inside these ranges and needn't reach their ends.
Inputs may be any that keep to these rules, and one draw needn't show every extreme that they name: `locality`: within each bas shard, its 16 orbital tiles name each of its 16 blocks exactly once.
All inputs are finite; a program needn't handle non-finite values. No bound on the sum of `screen` on one device may be relied on, other than what follows from the above.
Results may differ from the reference program's by a relative error of at most 0.00096.
Values may be sent and summed in bfloat16 or wider, within the bound.
No kernel may reach another device: no remote copies, remote signals or barrier semaphores. Data moves between devices by JAX's collectives and lax.ppermute only.
A program may use at most 128 MiB of HBM per device.

```python
import jax
import jax.numpy as jnp
from jax import lax

TILE = 128
W = 3
AUX_DEV = 1
OPD = 1
NAUX = 16
AUX_TILES = 16
BLK_DEV = 16
NBLK = 32
NORBT = 32
N_AUX = 16


def draw_metric(key, part):
    key_off, key_diag = jax.random.split(key)
    spread = 0.5
    upper_end = 2.0
    noise_part = jnp.clip(jax.random.normal(key_off, (NAUX, NAUX), jnp.float32), -4.0, 4.0) * (spread / NAUX ** 0.5)
    diag_values = jax.random.uniform(key_diag, (NAUX,), jnp.float32, 1.0, upper_end)
    on_diagonal = jnp.arange(NAUX)[:, None] == jnp.arange(NAUX)[None, :]
    return jnp.where(on_diagonal, diag_values[:, None], noise_part).astype(jnp.bfloat16)


def draw_locality(key, part):
    shard_keys = jax.random.split(jax.random.fold_in(key, 17), NBLK // BLK_DEV)
    orders = jax.vmap(lambda one_key: jax.random.permutation(one_key, BLK_DEV))(shard_keys)
    return orders.reshape(-1).astype(jnp.int32)


def place_ends(entries, rng, low, largest):
    spot = [jax.random.randint(jax.random.fold_in(rng, axis), (), 0, length) for axis, length in enumerate(entries.shape)]
    main_axis = entries.shape.index(max(entries.shape))
    beside = spot[:main_axis] + [(spot[main_axis] + 1) % entries.shape[main_axis]] + spot[main_axis + 1:]
    return entries.at[tuple(spot)].set(low).at[tuple(beside)].set(largest)


def level_of(rng, shape, pieces, smallest, top_value):
    level, own = 1.0, jax.random.fold_in(rng, 6)
    for dim, parts in pieces:
        steps = jnp.exp(jax.random.uniform(jax.random.fold_in(own, dim), (parts,), jnp.float32, smallest / len(pieces), top_value / len(pieces)))
        level = level * jnp.repeat(steps, shape[dim] // parts).reshape([-1 if axis == dim else 1 for axis in range(len(shape))])
    return level


def centred(rng, extent, scale, bound, cuts=(), held_as=jnp.bfloat16):
    array = scale * jax.random.normal(rng, extent, jnp.float32)
    if cuts:
        array = array * level_of(rng, extent, cuts, -0.22, 0.18)
    return jnp.clip(array, -bound, bound).astype(held_as)


def setup_inputs(seed: int = 0) -> dict:
    keys = jax.random.split(jax.random.key(seed), 6)
    integrals = centred(keys[0], (NAUX, NBLK, W, TILE, TILE), (1.0 / (720 * NAUX) ** 0.5), 0.125, ((0, 16), (1, 2)))
    orbitals = centred(keys[1], (NORBT, TILE, TILE), TILE ** -0.5, 0.5, ((0, 2),))
    locality = draw_locality(jax.random.fold_in(keys[5], 71), 0)
    screen = place_ends((jax.random.randint(keys[3], (AUX_TILES, NORBT, W), 0, 4) < 3).astype(jnp.int32), jax.random.fold_in(keys[3], 1), 0, 1)
    metric = draw_metric(jax.random.fold_in(keys[5], 71), 0)
    return {"integrals": integrals, "orbitals": orbitals, "locality": locality, "screen": screen, "metric": metric}


def reference(integrals, orbitals, locality, screen, metric):
    aux_count, block_count, reach_width, tile_size, _ = integrals.shape
    reach_blocks = reach_width // 2
    orbital_count = orbitals.shape[0]
    tile_ids = jnp.arange(orbital_count, dtype=jnp.int32)
    centres = ((tile_ids // (OPD * N_AUX)) * BLK_DEV + locality).astype(jnp.int32)
    aux_tiles = (jnp.arange(aux_count, dtype=jnp.int32) // AUX_DEV).astype(jnp.int32)
    offsets = jnp.arange(reach_width, dtype=jnp.int32)
    band_shape = (block_count + 2 * reach_blocks, 2 * reach_width - 1, tile_size, tile_size)

    def one_tile(band_sum, inputs):
        coefficients, centre_block, flag_rows = inputs
        chosen = lax.dynamic_index_in_dim(integrals, centre_block, axis=1, keepdims=False)
        half_rows = jnp.dot(chosen.reshape(-1, tile_size), coefficients, preferred_element_type=jnp.float32)
        half_rows = half_rows.reshape(aux_count, reach_width, tile_size, tile_size)
        row_blocks = centre_block + offsets - reach_blocks
        inside = ((row_blocks >= 0) & (row_blocks < block_count)).astype(jnp.float32)
        keep_mask = jnp.take(flag_rows, aux_tiles, axis=0).astype(jnp.float32) * inside[None, :]
        half_rows = (half_rows * keep_mask[:, :, None, None]).astype(jnp.bfloat16)
        mixed_rows = jnp.dot(metric, half_rows.reshape(aux_count, -1), preferred_element_type=jnp.float32)
        mixed_rows = mixed_rows.astype(jnp.bfloat16).reshape(half_rows.shape).astype(jnp.float32)
        gram_block = lax.dot_general(mixed_rows, mixed_rows, (((0, 3), (0, 3)), ((), ())))
        for offset in range(reach_width):
            band_piece = jnp.transpose(gram_block[offset], (1, 0, 2))
            band_piece = jnp.pad(band_piece, ((reach_width - 1 - offset, offset), (0, 0), (0, 0)))
            band_sum = band_sum.at[centre_block + offset].add(band_piece)
        return band_sum, None

    band_sum, _ = lax.scan(one_tile, jnp.zeros(band_shape, jnp.float32), (orbitals, centres, jnp.transpose(screen, (1, 0, 2))))
    result = band_sum[reach_blocks:reach_blocks + block_count]
    return result.reshape(block_count, 2 * reach_width - 1, tile_size * tile_size)
```

```python
import functools

import jax
import jax.numpy as jnp
from jax import lax
from jax.experimental import pallas as pl
from jax.experimental.pallas import tpu as pltpu
from jax.sharding import PartitionSpec as P

ROWS = 8
LEVELS = 32000.0
STEPS = 128.0
FAST = pltpu.CompilerParams(vmem_limit_bytes=48 * 1024 * 1024)


def half_kernel(locality, screen, integrals, orbitals, half, taken, given, in_sem, out_sem):
    tiles, reach, tile, _ = taken.shape
    total = tiles * lax.axis_size("bas")
    first = lax.axis_index("bas") * tiles

    def fetch(j):
        return pltpu.make_async_copy(integrals.at[0, locality[j]], taken.at[j], in_sem.at[j])

    def give(j):
        return pltpu.make_async_copy(given.at[j], half.at[locality[j]], out_sem.at[j])

    for j in range(tiles):
        fetch(j).start()
    for j in range(tiles):
        fetch(j).wait()
        product = jnp.dot(
            taken[j].reshape(reach * tile, tile), orbitals[j], preferred_element_type=jnp.float32
        )
        for d in range(reach):
            block = first + locality[j] + d - reach // 2
            inside = (block >= 0) & (block < total)
            keep = jnp.where(inside, screen[0, j, d], 0).astype(jnp.float32)
            given[j, d] = (product[d * tile : (d + 1) * tile] * keep).astype(jnp.bfloat16)
        give(j).start()
    for j in range(tiles):
        give(j).wait()


def gram_kernel(metric, rows, coded, taken, fitted, in_sem):
    aux, reach, tile, _ = taken.shape
    group = 16

    def fetch(d):
        return pltpu.make_async_copy(rows.at[:, d], taken.at[:, d], in_sem.at[d])

    for d in range(reach):
        fetch(d).start()
    wide = aux * group
    spread = (
        lax.broadcasted_iota(jnp.int32, (wide, aux), 0) // group
        == lax.broadcasted_iota(jnp.int32, (wide, aux), 1)
    ).astype(jnp.bfloat16)
    picked = jnp.dot(spread, metric[...], preferred_element_type=jnp.float32).astype(jnp.bfloat16)
    mixer = lax.dot_general(
        picked, spread, (((1,), (1,)), ((), ())), preferred_element_type=jnp.float32
    )
    same_row = (
        lax.broadcasted_iota(jnp.int32, (wide, wide), 0) % group
        == lax.broadcasted_iota(jnp.int32, (wide, wide), 1) % group
    )
    mixer = jnp.where(same_row, mixer, 0.0).astype(jnp.bfloat16)
    for d in range(reach):
        fetch(d).wait()
        for g in range(0, tile, 2 * group):
            pair = [
                taken[:, d, g + s * group : g + (s + 1) * group, :].reshape(wide, tile)
                for s in range(2)
            ]
            mixed = jnp.dot(
                mixer, jnp.concatenate(pair, axis=1), preferred_element_type=jnp.float32
            ).astype(jnp.bfloat16)
            for s in range(2):
                start = d * tile + g + s * group
                for q in range(aux):
                    fitted[start : start + group, q * tile : (q + 1) * tile] = mixed[
                        q * group : (q + 1) * group, s * tile : (s + 1) * tile
                    ]
    gram = lax.dot_general(
        fitted[...], fitted[...], (((1,), (1,)), ((), ())), preferred_element_type=jnp.float32
    )
    lane = lax.broadcasted_iota(jnp.int32, (ROWS, tile), 1)
    owners = coded.shape[0]
    per = tile // owners
    for a in range(owners):
        codes, scales = [], jnp.zeros((ROWS, tile), jnp.float32)
        for d in range(reach):
            for d2 in range(reach):
                block = gram[
                    d * tile + a * per : d * tile + (a + 1) * per, d2 * tile : (d2 + 1) * tile
                ]
                if per < ROWS:
                    block = jnp.concatenate(
                        [block, jnp.zeros((ROWS - per, tile), jnp.float32)], axis=0
                    )
                code, scale = encode(block)
                codes.append(code)
                scales = jnp.where(lane == d * reach + d2, scale, scales)
        sent = jnp.concatenate(codes + [scales], axis=0)
        coded[a] = sent.astype(jnp.int32).astype(jnp.int16)


def encode(block):
    peak = jnp.max(jnp.abs(block), axis=1, keepdims=True)
    scale = jnp.ceil(jnp.log2(jnp.maximum(peak, 1e-37)) * STEPS)
    return jnp.round(block * (jnp.exp2(scale * (-1.0 / STEPS)) * LEVELS)), scale


def decode(codes, scales, which):
    factor = jnp.exp2(scales[:, which : which + 1] * (1.0 / STEPS)) * (1.0 / LEVELS)
    return codes[which * ROWS : (which + 1) * ROWS] * factor


def band_kernel(reach, received, rim, band):
    centres, height, tile = received.shape
    per = band.shape[2] // tile
    offsets = 2 * reach - 1
    middle = reach // 2
    on_first = lax.axis_index("bas") == 0
    sums = {}

    def add(m, e, piece):
        sums[m, e] = sums[m, e] + piece if (m, e) in sums else piece

    def finish(m):
        for e in range(offsets):
            total = sums.pop((m, e), jnp.zeros((ROWS, tile), jnp.float32))
            for r in range(per):
                band[m, e : e + 1, r * tile : (r + 1) * tile] = total[r : r + 1]

    beside = rim[0].astype(jnp.int32).astype(jnp.float32)
    beside_scales = beside[reach * reach * ROWS :]
    for d2 in range(reach):
        low = decode(beside, beside_scales, (reach - 1) * reach + d2)
        add(0, d2, jnp.where(on_first, 0.0, low))
        high = decode(beside, beside_scales, d2)
        add(centres - 1, d2 + reach - 1, jnp.where(on_first, high, 0.0))
    for c in range(centres):
        tile_codes = received[c].astype(jnp.int32).astype(jnp.float32)
        scales = tile_codes[reach * reach * ROWS :]
        for d in range(reach):
            m = c + d - middle
            if 0 <= m < centres:
                for d2 in range(reach):
                    add(m, d2 - d + reach - 1, decode(tile_codes, scales, d * reach + d2))
        if c >= middle:
            finish(c - middle)
    for m in range(centres - middle, centres):
        finish(m)


def body(integrals, orbitals, locality, screen, metric):
    _, tiles, reach, tile, _ = integrals.shape
    aux = lax.axis_size("aux")
    if lax.axis_size("bas") != 2 or tiles != aux or reach != 3:
        raise ValueError("unsupported sizes")
    any_space = pl.BlockSpec(memory_space=pl.ANY)
    scalars = pl.BlockSpec(memory_space=pltpu.SMEM)
    vectors = pl.BlockSpec(memory_space=pltpu.VMEM)
    half = pl.pallas_call(
        half_kernel,
        out_shape=jax.ShapeDtypeStruct((tiles, reach, tile, tile), jnp.bfloat16),
        in_specs=[scalars, scalars, any_space, vectors],
        out_specs=any_space,
        scratch_shapes=[
            pltpu.VMEM((tiles, reach, tile, tile), jnp.bfloat16),
            pltpu.VMEM((tiles, reach, tile, tile), jnp.bfloat16),
            pltpu.SemaphoreType.DMA((tiles,)),
            pltpu.SemaphoreType.DMA((tiles,)),
        ],
        compiler_params=FAST,
        name="half_transform",
    )(locality, screen, integrals, orbitals)
    rows = lax.all_to_all(half, "aux", split_axis=0, concat_axis=0, tiled=True)
    coded = pl.pallas_call(
        gram_kernel,
        out_shape=jax.ShapeDtypeStruct((aux, (reach * reach + 1) * ROWS, tile), jnp.int16),
        in_specs=[vectors, any_space],
        out_specs=vectors,
        scratch_shapes=[
            pltpu.VMEM((aux, reach, tile, tile), jnp.bfloat16),
            pltpu.VMEM((reach * tile, aux * tile), jnp.bfloat16),
            pltpu.SemaphoreType.DMA((reach,)),
        ],
        compiler_params=FAST,
        name="fit_and_gram",
    )(metric, rows)
    received = lax.all_to_all(coded, "aux", split_axis=0, concat_axis=0, tiled=True)
    edge = jnp.where(lax.axis_index("bas") == 0, tiles - 1, 0)
    edge_tile = lax.dynamic_slice_in_dim(received, edge, 1, 0)
    rim = lax.ppermute(edge_tile, "bas", [(0, 1), (1, 0)])
    return pl.pallas_call(
        functools.partial(band_kernel, reach),
        out_shape=jax.ShapeDtypeStruct(
            (tiles, 2 * reach - 1, tile * tile // aux), jnp.float32
        ),
        in_specs=[vectors, vectors],
        out_specs=vectors,
        compiler_params=FAST,
        name="band_sum",
    )(received, rim)


def solution(mesh):
    placed = (
        P("aux", "bas", None, None, None),
        P("bas", None, None),
        P("bas"),
        P("aux", "bas", None),
        P(),
    )
    return jax.shard_map(
        body, mesh=mesh, in_specs=placed, out_specs=P("bas", None, "aux"), check_vma=False
    )
```

```python
import functools

import jax
import jax.numpy as jnp
from jax import lax
from jax.experimental import pallas as pl
from jax.experimental.pallas import tpu as pltpu
from jax.sharding import PartitionSpec as P

ROWS = 8
LEVELS = 32000.0
PARTS = 4
STEPS = 128.0
FAST = pltpu.CompilerParams(vmem_limit_bytes=48 * 1024 * 1024)


def half_kernel(
    locality, screen, integrals, orbitals, half, taken, factors, places, flags, owner, sems
):
    tiles, reach, tile, _ = taken.shape
    total = tiles * lax.axis_size("bas")
    first = lax.axis_index("bas") * tiles
    part = max(tiles // PARTS, 1)
    small = [
        pltpu.make_async_copy(locality, places, sems.at[0]),
        pltpu.make_async_copy(screen, flags, sems.at[1]),
        pltpu.make_async_copy(orbitals, factors, sems.at[2]),
    ]
    blocks = [
        pltpu.make_async_copy(
            integrals.at[0, pl.ds(start, part)], taken.at[pl.ds(start, part)], sems.at[3 + k]
        )
        for k, start in enumerate(range(0, tiles, part))
    ]
    for copy in small + blocks:
        copy.start()
    small[0].wait()
    for j in range(tiles):
        owner[places[j]] = j
    small[1].wait()
    small[2].wait()
    for k, copy in enumerate(blocks):
        copy.wait()
        for c in range(k * part, (k + 1) * part):
            j = owner[c]
            product = jnp.dot(
                taken[c].reshape(reach * tile, tile),
                factors[j],
                preferred_element_type=jnp.float32,
            )
            for d in range(reach):
                block = first + c + d - reach // 2
                inside = (block >= 0) & (block < total)
                keep = jnp.where(inside, flags[d, 0, j], 0).astype(jnp.float32)
                half[c, d] = (product[d * tile : (d + 1) * tile] * keep).astype(jnp.bfloat16)


def gram_kernel(metric, rows, coded, fitted):
    aux, reach, tile, _ = rows.shape
    group = 16
    wide = aux * group
    spread = (
        lax.broadcasted_iota(jnp.int32, (wide, aux), 0) // group
        == lax.broadcasted_iota(jnp.int32, (wide, aux), 1)
    ).astype(jnp.bfloat16)
    picked = jnp.dot(spread, metric[...], preferred_element_type=jnp.float32).astype(jnp.bfloat16)
    mixer = lax.dot_general(
        picked, spread, (((1,), (1,)), ((), ())), preferred_element_type=jnp.float32
    )
    same_row = (
        lax.broadcasted_iota(jnp.int32, (wide, wide), 0) % group
        == lax.broadcasted_iota(jnp.int32, (wide, wide), 1) % group
    )
    mixer = jnp.where(same_row, mixer, 0.0).astype(jnp.bfloat16)
    for d in range(reach):
        for g in range(0, tile, 2 * group):
            pair = [
                rows[:, d, g + s * group : g + (s + 1) * group, :].reshape(wide, tile)
                for s in range(2)
            ]
            mixed = jnp.dot(
                mixer, jnp.concatenate(pair, axis=1), preferred_element_type=jnp.float32
            ).astype(jnp.bfloat16)
            for s in range(2):
                start = d * tile + g + s * group
                for q in range(aux):
                    fitted[start : start + group, q * tile : (q + 1) * tile] = mixed[
                        q * group : (q + 1) * group, s * tile : (s + 1) * tile
                    ]
    gram = lax.dot_general(
        fitted[...], fitted[...], (((1,), (1,)), ((), ())), preferred_element_type=jnp.float32
    )
    lane = lax.broadcasted_iota(jnp.int32, (ROWS, tile), 1)
    owners = coded.shape[0]
    per = tile // owners
    for a in range(owners):
        codes, scales = [], jnp.zeros((ROWS, tile), jnp.float32)
        for d in range(reach):
            for d2 in range(reach):
                block = gram[
                    d * tile + a * per : d * tile + (a + 1) * per, d2 * tile : (d2 + 1) * tile
                ]
                if per < ROWS:
                    block = jnp.concatenate(
                        [block, jnp.zeros((ROWS - per, tile), jnp.float32)], axis=0
                    )
                code, scale = encode(block)
                codes.append(code)
                scales = jnp.where(lane == d * reach + d2, scale, scales)
        sent = jnp.concatenate(codes + [scales], axis=0)
        coded[a] = sent.astype(jnp.int32).astype(jnp.int16)


def encode(block):
    peak = jnp.max(jnp.abs(block), axis=1, keepdims=True)
    scale = jnp.ceil(jnp.log2(jnp.maximum(peak, 1e-37)) * STEPS)
    return jnp.round(block * (jnp.exp2(scale * (-1.0 / STEPS)) * LEVELS)), scale


def decode(codes, scales, which):
    factor = jnp.exp2(scales[:, which : which + 1] * (1.0 / STEPS)) * (1.0 / LEVELS)
    return codes[which * ROWS : (which + 1) * ROWS] * factor


def band_kernel(reach, received, rim, band):
    centres, _, tile = received.shape
    per = band.shape[2] // tile
    offsets = 2 * reach - 1
    middle = reach // 2
    on_first = lax.axis_index("bas") == 0
    sums = {}

    def add(m, e, piece):
        sums[m, e] = sums[m, e] + piece if (m, e) in sums else piece

    def finish(m):
        for e in range(offsets):
            total = sums.pop((m, e), jnp.zeros((ROWS, tile), jnp.float32))
            for r in range(per):
                band[e, m : m + 1, r * tile : (r + 1) * tile] = total[r : r + 1]

    beside = rim[0].astype(jnp.int32).astype(jnp.float32)
    beside_scales = beside[reach * reach * ROWS :]
    for d2 in range(reach):
        low = decode(beside, beside_scales, (reach - 1) * reach + d2)
        add(0, d2, jnp.where(on_first, 0.0, low))
        high = decode(beside, beside_scales, d2)
        add(centres - 1, d2 + reach - 1, jnp.where(on_first, high, 0.0))
    for c in range(centres):
        tile_codes = received[c].astype(jnp.int32).astype(jnp.float32)
        scales = tile_codes[reach * reach * ROWS :]
        for d in range(reach):
            m = c + d - middle
            if 0 <= m < centres:
                for d2 in range(reach):
                    add(m, d2 - d + reach - 1, decode(tile_codes, scales, d * reach + d2))
        if c >= middle:
            finish(c - middle)
    for m in range(centres - middle, centres):
        finish(m)


def body(integrals, orbitals, locality, screen, metric):
    _, tiles, reach, tile, _ = integrals.shape
    aux = lax.axis_size("aux")
    if lax.axis_size("bas") != 2 or tiles != aux or reach != 3:
        raise ValueError("unsupported sizes")
    main_memory = pl.BlockSpec(memory_space=pltpu.HBM)
    vectors = pl.BlockSpec(memory_space=pltpu.VMEM)
    half = pl.pallas_call(
        half_kernel,
        out_shape=jax.ShapeDtypeStruct((tiles, reach, tile, tile), jnp.bfloat16),
        in_specs=[main_memory] * 4,
        out_specs=vectors,
        scratch_shapes=[
            pltpu.VMEM((tiles, reach, tile, tile), jnp.bfloat16),
            pltpu.VMEM((tiles, tile, tile), jnp.bfloat16),
            pltpu.SMEM((tiles,), jnp.int32),
            pltpu.SMEM((reach, 1, tiles), jnp.int32),
            pltpu.SMEM((tiles,), jnp.int32),
            pltpu.SemaphoreType.DMA((3 + PARTS,)),
        ],
        compiler_params=FAST,
        name="half_transform",
    )(*(
        pltpu.with_memory_space_constraint(array, pltpu.HBM)
        for array in (locality, jnp.transpose(screen, (2, 0, 1)), integrals, orbitals)
    ))
    rows = lax.all_to_all(half, "aux", split_axis=0, concat_axis=0, tiled=True)
    coded = pl.pallas_call(
        gram_kernel,
        out_shape=jax.ShapeDtypeStruct((aux, (reach * reach + 1) * ROWS, tile), jnp.int16),
        in_specs=[vectors, vectors],
        out_specs=vectors,
        scratch_shapes=[
            pltpu.VMEM((reach * tile, aux * tile), jnp.bfloat16),
        ],
        compiler_params=FAST,
        name="fit_and_gram",
    )(metric, rows)
    received = lax.all_to_all(coded, "aux", split_axis=0, concat_axis=0, tiled=True)
    edge = jnp.where(lax.axis_index("bas") == 0, tiles - 1, 0)
    edge_tile = lax.dynamic_slice_in_dim(received, edge, 1, 0)
    rim = lax.ppermute(edge_tile, "bas", [(0, 1), (1, 0)])
    band = pl.pallas_call(
        functools.partial(band_kernel, reach),
        out_shape=jax.ShapeDtypeStruct(
            (2 * reach - 1, tiles, tile * tile // aux), jnp.float32
        ),
        in_specs=[vectors, vectors],
        out_specs=vectors,
        compiler_params=FAST,
        name="band_sum",
    )(received, rim)
    return jnp.transpose(band, (1, 0, 2))


def solution(mesh):
    placed = (
        P("aux", "bas", None, None, None),
        P("bas", None, None),
        P("bas"),
        P("aux", "bas", None),
        P(),
    )
    return jax.shard_map(
        body, mesh=mesh, in_specs=placed, out_specs=P("bas", None, "aux"), check_vma=False
    )
```

```python
import functools

import jax
import jax.numpy as jnp
from jax import lax
from jax.experimental import pallas as pl
from jax.experimental.pallas import tpu as pltpu
from jax.sharding import PartitionSpec as P

ROWS = 8
LEVELS = 32000.0
WINDOW = 4
PATTERN = "FFFNFNFNFNNFNNF"
PARTS = 4
STEPS = 128.0
FAST = pltpu.CompilerParams(vmem_limit_bytes=48 * 1024 * 1024)


def half_kernel(crossing, locality, screen, integrals, orbitals, *rest):
    *halves, taken, factors, places, flags, owner, sems = rest
    halves = halves[-taken.shape[0] :]
    count, reach, tile, _ = taken.shape
    tiles = 2 * count
    me = lax.axis_index("aux")
    order = [me ^ (count * crossing + k) for k in range(count)]
    total = tiles * lax.axis_size("bas")
    first = lax.axis_index("bas") * tiles
    part = max(count // PARTS, 1)
    small = [
        pltpu.make_async_copy(locality, places, sems.at[0]),
        pltpu.make_async_copy(screen, flags, sems.at[1]),
        pltpu.make_async_copy(orbitals, factors, sems.at[2]),
    ]
    blocks = [
        pltpu.make_async_copy(integrals.at[0, centre], taken.at[k], sems.at[3 + k])
        for k, centre in enumerate(order)
    ]
    for copy in small + blocks:
        copy.start()
    small[0].wait()
    for j in range(tiles):
        owner[places[j]] = j
    small[1].wait()
    small[2].wait()
    for k, centre in enumerate(order):
        if k % part == 0:
            for copy in blocks[k : k + part]:
                copy.wait()
        j = owner[centre]
        product = jnp.dot(
            taken[k].reshape(reach * tile, tile), factors[j], preferred_element_type=jnp.float32
        )
        for d in range(reach):
            block = first + centre + d - reach // 2
            inside = (block >= 0) & (block < total)
            keep = jnp.where(inside, flags[d, 0, j], 0).astype(jnp.float32)
            kept = (product[d * tile : (d + 1) * tile] * keep).astype(jnp.bfloat16)
            halves[k][d] = kept


def gram_kernel(metric, *rest):
    *pieces, coded, fitted = rest
    aux = len(pieces)
    reach, tile, _ = pieces[0].shape
    me = lax.axis_index("aux")
    group = 16
    wide = aux * group
    spread = (
        lax.broadcasted_iota(jnp.int32, (wide, aux), 0) // group
        == lax.broadcasted_iota(jnp.int32, (wide, aux), 1)
    ).astype(jnp.bfloat16)
    picked = jnp.dot(spread, metric[...], preferred_element_type=jnp.float32).astype(jnp.bfloat16)
    slot = lax.broadcasted_iota(jnp.int32, (wide, aux), 0) // group
    from_slot = ((me ^ slot) == lax.broadcasted_iota(jnp.int32, (wide, aux), 1)).astype(jnp.bfloat16)
    mixer = lax.dot_general(
        picked, from_slot, (((1,), (1,)), ((), ())), preferred_element_type=jnp.float32
    )
    same_row = (
        lax.broadcasted_iota(jnp.int32, (wide, wide), 0) % group
        == lax.broadcasted_iota(jnp.int32, (wide, wide), 1) % group
    )
    mixer = jnp.where(same_row, mixer, 0.0).astype(jnp.bfloat16)
    for d in range(reach):
        for g in range(0, tile, 2 * group):
            pair = []
            for start in (g, g + group):
                here = slice(start, start + group)
                pair.append(jnp.concatenate([piece[d, here, :] for piece in pieces], axis=0))
            mixed = jnp.dot(
                mixer, jnp.concatenate(pair, axis=1), preferred_element_type=jnp.float32
            ).astype(jnp.bfloat16)
            for s in range(2):
                start = d * tile + g + s * group
                for q in range(aux):
                    fitted[start : start + group, q * tile : (q + 1) * tile] = mixed[
                        q * group : (q + 1) * group, s * tile : (s + 1) * tile
                    ]
    gram = lax.dot_general(
        fitted[...], fitted[...], (((1,), (1,)), ((), ())), preferred_element_type=jnp.float32
    )
    lane = lax.broadcasted_iota(jnp.int32, (ROWS, tile), 1)
    owners = coded.shape[0]
    per = tile // owners
    for a in range(owners):
        codes, scales = [], jnp.zeros((ROWS, tile), jnp.float32)
        for d in range(reach):
            for d2 in range(reach):
                block = gram[
                    d * tile + a * per : d * tile + (a + 1) * per, d2 * tile : (d2 + 1) * tile
                ]
                if per < ROWS:
                    block = jnp.concatenate(
                        [block, jnp.zeros((ROWS - per, tile), jnp.float32)], axis=0
                    )
                code, scale = encode(block)
                codes.append(code)
                scales = jnp.where(lane == d * reach + d2, scale, scales)
        sent = jnp.concatenate(codes + [scales], axis=0)
        coded[a] = sent.astype(jnp.int32).astype(jnp.int16)


def encode(block):
    peak = jnp.max(jnp.abs(block), axis=1, keepdims=True)
    scale = jnp.ceil(jnp.log2(jnp.maximum(peak, 1e-37)) * STEPS)
    return jnp.round(block * (jnp.exp2(scale * (-1.0 / STEPS)) * LEVELS)), scale


def decode(codes, scales, which):
    factor = jnp.exp2(scales[:, which : which + 1] * (1.0 / STEPS)) * (1.0 / LEVELS)
    return codes[which * ROWS : (which + 1) * ROWS] * factor


def band_kernel(reach, received, rim, band):
    centres, _, tile = received.shape
    per = band.shape[2] // tile
    offsets = 2 * reach - 1
    middle = reach // 2
    on_first = lax.axis_index("bas") == 0
    sums = {}

    def add(m, e, piece):
        sums[m, e] = sums[m, e] + piece if (m, e) in sums else piece

    def finish(m):
        for e in range(offsets):
            total = sums.pop((m, e), jnp.zeros((ROWS, tile), jnp.float32))
            for r in range(per):
                band[e, m : m + 1, r * tile : (r + 1) * tile] = total[r : r + 1]

    beside = rim[0].astype(jnp.int32).astype(jnp.float32)
    beside_scales = beside[reach * reach * ROWS :]
    for d2 in range(reach):
        low = decode(beside, beside_scales, (reach - 1) * reach + d2)
        add(0, d2, jnp.where(on_first, 0.0, low))
        high = decode(beside, beside_scales, d2)
        add(centres - 1, d2 + reach - 1, jnp.where(on_first, high, 0.0))
    for c in range(centres):
        tile_codes = received[c].astype(jnp.int32).astype(jnp.float32)
        scales = tile_codes[reach * reach * ROWS :]
        for d in range(reach):
            m = c + d - middle
            if 0 <= m < centres:
                for d2 in range(reach):
                    add(m, d2 - d + reach - 1, decode(tile_codes, scales, d * reach + d2))
        if c >= middle:
            finish(c - middle)
    for m in range(centres - middle, centres):
        finish(m)


def body(integrals, orbitals, locality, screen, metric):
    _, tiles, reach, tile, _ = integrals.shape
    aux = lax.axis_size("aux")
    if lax.axis_size("bas") != 2 or tiles != aux or aux & (aux - 1) or reach != 3:
        raise ValueError("unsupported sizes")
    main_memory = pl.BlockSpec(memory_space=pltpu.HBM)
    vectors = pl.BlockSpec(memory_space=pltpu.VMEM)
    half = aux // 2
    inputs = [
        pltpu.with_memory_space_constraint(array, pltpu.HBM)
        for array in (locality, jnp.transpose(screen, (2, 0, 1)), integrals, orbitals)
    ]
    scratch = [
        pltpu.VMEM((half, reach, tile, tile), jnp.bfloat16),
        pltpu.VMEM((tiles, tile, tile), jnp.bfloat16),
        pltpu.SMEM((tiles,), jnp.int32),
        pltpu.SMEM((reach, 1, tiles), jnp.int32),
        pltpu.SMEM((tiles,), jnp.int32),
        pltpu.SemaphoreType.DMA((3 + half,)),
    ]
    far = pl.pallas_call(
        functools.partial(half_kernel, True),
        out_shape=[jax.ShapeDtypeStruct((reach, tile, tile), jnp.bfloat16)] * half,
        in_specs=[main_memory] * 4,
        out_specs=[vectors] * half,
        scratch_shapes=scratch,
        compiler_params=FAST,
        name="half_far",
    )(*inputs)
    near = pl.pallas_call(
        functools.partial(half_kernel, False),
        out_shape=[jax.ShapeDtypeStruct((reach, tile, tile), jnp.bfloat16)] * half,
        in_specs=[main_memory] * 4 + [pl.BlockSpec(memory_space=pl.ANY)],
        out_specs=[vectors] * half,
        scratch_shapes=scratch,
        compiler_params=FAST,
        name="half_near",
    )(*inputs, far[0])
    pieces = near + far
    moved = {0: pieces[0]}
    order = exchange_order(aux)
    for t, k in enumerate(order):
        piece = pieces[k]
        if t >= WINDOW:
            piece, _ = lax.optimization_barrier((piece, moved[order[t - WINDOW]]))
        moved[k] = lax.ppermute(piece, "aux", [(i, i ^ k) for i in range(aux)])
    pieces = [moved[k] for k in range(aux)]
    coded = pl.pallas_call(
        gram_kernel,
        out_shape=jax.ShapeDtypeStruct((aux, (reach * reach + 1) * ROWS, tile), jnp.int16),
        in_specs=[vectors] * (aux + 1),
        out_specs=vectors,
        scratch_shapes=[
            pltpu.VMEM((reach * tile, aux * tile), jnp.bfloat16),
        ],
        compiler_params=FAST,
        name="fit_and_gram",
    )(metric, *pieces)
    received = lax.all_to_all(coded, "aux", split_axis=0, concat_axis=0, tiled=True)
    edge = jnp.where(lax.axis_index("bas") == 0, tiles - 1, 0)
    edge_tile = lax.dynamic_slice_in_dim(received, edge, 1, 0)
    rim = lax.ppermute(edge_tile, "bas", [(0, 1), (1, 0)])
    band = pl.pallas_call(
        functools.partial(band_kernel, reach),
        out_shape=jax.ShapeDtypeStruct(
            (2 * reach - 1, tiles, tile * tile // aux), jnp.float32
        ),
        in_specs=[vectors, vectors],
        out_specs=vectors,
        compiler_params=FAST,
        name="band_sum",
    )(received, rim)
    return jnp.transpose(band, (1, 0, 2))


def exchange_order(devices):
    half = devices // 2
    far = [half + i // 2 + i % 2 * (half // 2) for i in range(half)]
    near = list(range(half - 1, 0, -1))
    turns = PATTERN if len(PATTERN) == devices - 1 else "F" + "FN" * (half - 1)
    return [far.pop(0) if turn == "F" else near.pop(0) for turn in turns]


def solution(mesh):
    placed = (
        P("aux", "bas", None, None, None),
        P("bas", None, None),
        P("bas"),
        P("aux", "bas", None),
        P(),
    )
    return jax.shard_map(
        body, mesh=mesh, in_specs=placed, out_specs=P("bas", None, "aux"), check_vma=False
    )
```

```python
import functools

import jax
import jax.numpy as jnp
from jax import lax
from jax.experimental import pallas as pl
from jax.experimental.pallas import tpu as pltpu
from jax.sharding import PartitionSpec as P

ROWS = 8
LEVELS = 32000.0
GROUP = 16
HEAD = 8
ORDERS = (
    [8, 13, 7, 6, 9, 5, 12, 4, 10, 3, 2, 14, 11, 1, 15],
    [10, 5, 11, 7, 15, 6, 8, 14, 12, 1, 3, 9, 2, 4, 13],
)
WINDOWS = [4] * 15
PARTS = 2
STEPS = 128.0
FAST = pltpu.CompilerParams(vmem_limit_bytes=48 * 1024 * 1024)


def exchange_orders(devices):
    if devices - 1 == len(ORDERS[0]):
        return ORDERS
    half = devices // 2
    order = [half]
    for k in range(1, half):
        order += [k, half + k]
    return order, order


def partner(t):
    first, second = exchange_orders(lax.axis_size("aux"))
    return jnp.where(lax.axis_index("bas") == 0, first[t], second[t])


def half_kernel(slots, locality, screen, integrals, orbitals, *rest):
    *halves, taken, factors, places, flags, owner, sems = rest
    if slots[-1] is None:
        metric, _, *halves, mixer = halves
    count, reach, tile, _ = taken.shape
    tiles = factors.shape[0]
    me = lax.axis_index("aux")
    order = [me if t is None else me ^ partner(t) for t in slots]
    total = tiles * lax.axis_size("bas")
    first = lax.axis_index("bas") * tiles
    part = max(count // PARTS, 1)
    small = [
        pltpu.make_async_copy(locality, places, sems.at[0]),
        pltpu.make_async_copy(screen, flags, sems.at[1]),
        pltpu.make_async_copy(orbitals, factors, sems.at[2]),
    ]
    blocks = [
        pltpu.make_async_copy(integrals.at[0, centre], taken.at[k], sems.at[3 + k])
        for k, centre in enumerate(order)
    ]
    for copy in small + blocks:
        copy.start()
    small[0].wait()
    for j in range(tiles):
        owner[places[j]] = j
    small[1].wait()
    small[2].wait()
    if slots[-1] is None:
        write_mixer(metric, mixer)
    for k, centre in enumerate(order):
        if k % part == 0:
            for copy in blocks[k : k + part]:
                copy.wait()
        j = owner[centre]
        product = jnp.dot(
            taken[k].reshape(reach * tile, tile), factors[j], preferred_element_type=jnp.float32
        )
        for d in range(reach):
            block = first + centre + d - reach // 2
            inside = (block >= 0) & (block < total)
            keep = jnp.where(inside, flags[d, 0, j], 0).astype(jnp.float32)
            kept = (product[d * tile : (d + 1) * tile] * keep).astype(jnp.bfloat16)
            halves[k][d] = kept


def write_mixer(metric, mixer):
    aux = metric.shape[0]
    wide = mixer.shape[0]
    group = wide // aux
    me = lax.axis_index("aux")
    slot = lax.broadcasted_iota(jnp.int32, (aux, aux), 0)
    came = jnp.full((aux, aux), me, jnp.int32)
    for t in range(aux - 1):
        came = jnp.where(slot == t + 1, me ^ partner(t), came)
    from_slot = (came == lax.broadcasted_iota(jnp.int32, (aux, aux), 1)).astype(jnp.bfloat16)
    placed = lax.dot_general(
        metric[...], from_slot, (((1,), (1,)), ((), ())), preferred_element_type=jnp.float32
    ).astype(jnp.bfloat16)
    spread = (
        lax.broadcasted_iota(jnp.int32, (wide, aux), 0) // group
        == lax.broadcasted_iota(jnp.int32, (wide, aux), 1)
    ).astype(jnp.bfloat16)
    picked = jnp.dot(spread, placed, preferred_element_type=jnp.float32).astype(jnp.bfloat16)
    full = lax.dot_general(
        picked, spread, (((1,), (1,)), ((), ())), preferred_element_type=jnp.float32
    )
    same_row = (
        lax.broadcasted_iota(jnp.int32, (wide, wide), 0) % group
        == lax.broadcasted_iota(jnp.int32, (wide, wide), 1) % group
    )
    mixer[...] = jnp.where(same_row, full, 0.0).astype(jnp.bfloat16)


def gram_kernel(mixer, *rest):
    *pieces, coded, fitted = rest
    aux = len(pieces)
    reach, tile, _ = pieces[0].shape
    group = GROUP
    wide = aux * group
    for d in range(reach):
        for g in range(0, tile, 2 * group):
            pair = []
            for start in (g, g + group):
                here = slice(start, start + group)
                pair.append(jnp.concatenate([piece[d, here, :] for piece in pieces], axis=0))
            mixed = jnp.dot(
                mixer[...], jnp.concatenate(pair, axis=1), preferred_element_type=jnp.float32
            ).astype(jnp.bfloat16)
            for s in range(2):
                start = d * tile + g + s * group
                for q in range(aux):
                    fitted[start : start + group, q * tile : (q + 1) * tile] = mixed[
                        q * group : (q + 1) * group, s * tile : (s + 1) * tile
                    ]
    gram = lax.dot_general(
        fitted[...], fitted[...], (((1,), (1,)), ((), ())), preferred_element_type=jnp.float32
    )
    lane = lax.broadcasted_iota(jnp.int32, (ROWS, tile), 1)
    owners = coded.shape[0]
    per = tile // owners
    for a in range(owners):
        codes, scales = [], jnp.zeros((ROWS, tile), jnp.float32)
        for d in range(reach):
            rows = gram[d * tile + a * per : d * tile + (a + 1) * per]
            if per < ROWS:
                rows = jnp.pad(rows, ((0, ROWS - per), (0, 0)))
            code, scale = encode(rows)
            codes += [code[:, d2 * tile : (d2 + 1) * tile] for d2 in range(reach)]
            scales = jnp.where(lane == d, scale, scales)
        sent = jnp.concatenate(codes + [scales], axis=0)
        coded[a] = sent.astype(jnp.int32).astype(jnp.int16)


def encode(rows):
    peak = jnp.max(jnp.abs(rows), axis=1, keepdims=True)
    scale = jnp.ceil(jnp.log2(jnp.maximum(peak, 1e-37)) * STEPS)
    return jnp.round(rows * jnp.exp2(scale * (-1.0 / STEPS)) * LEVELS), scale


def decode(sent, reach):
    sent = sent.astype(jnp.int32).astype(jnp.float32)
    scales = sent[reach * reach * ROWS :]
    blocks = []
    for d in range(reach):
        factor = jnp.exp2(scales[:, d : d + 1] * (1.0 / STEPS))
        starts = [(d * reach + d2) * ROWS for d2 in range(reach)]
        blocks.append([sent[i : i + ROWS] * (1.0 / LEVELS) * factor for i in starts])
    return blocks


def band_kernel(reach, received, band):
    centres, _, tile = received.shape
    per = band.shape[2] // tile
    offsets = 2 * reach - 1
    middle = reach // 2
    sums = {}

    def finish(m):
        for e in range(offsets):
            total = sums.pop((m, e), jnp.zeros((ROWS, tile), jnp.float32))
            for r in range(per):
                band[e, m : m + 1, r * tile : (r + 1) * tile] = total[r : r + 1]

    for c in range(centres):
        blocks = decode(received[c], reach)
        for d in range(reach):
            m = c + d - middle
            if 0 <= m < centres:
                for d2 in range(reach):
                    key = m, d2 - d + reach - 1
                    piece = blocks[d][d2]
                    sums[key] = sums[key] + piece if key in sums else piece
        if c >= middle:
            finish(c - middle)
    for m in range(centres - middle, centres):
        finish(m)


def rim_kernel(reach, part, rim, band):
    band[...] = part[...]
    tile = rim.shape[2]
    per = band.shape[2] // tile
    blocks = decode(rim[0], reach)

    def add(m, d, first):
        for d2 in range(reach):
            for r in range(per):
                here = first + d2, slice(m, m + 1), slice(r * tile, (r + 1) * tile)
                band[here] += blocks[d][d2][r : r + 1]

    @pl.when(lax.axis_index("bas") == 0)
    def _():
        add(band.shape[1] - 1, 0, reach - 1)

    @pl.when(lax.axis_index("bas") != 0)
    def _():
        add(0, reach - 1, 0)


def body(integrals, orbitals, locality, screen, metric):
    _, tiles, reach, tile, _ = integrals.shape
    aux = lax.axis_size("aux")
    if lax.axis_size("bas") != 2 or tiles != aux or aux & (aux - 1) or reach != 3:
        raise ValueError("unsupported sizes")
    main_memory = pl.BlockSpec(memory_space=pltpu.HBM)
    vectors = pl.BlockSpec(memory_space=pltpu.VMEM)
    inputs = [
        pltpu.with_memory_space_constraint(array, pltpu.HBM)
        for array in (locality, jnp.transpose(screen, (2, 0, 1)), integrals, orbitals)
    ]

    def half_rows(slots, more, out_shape, name):
        return pl.pallas_call(
            functools.partial(half_kernel, slots),
            out_shape=[jax.ShapeDtypeStruct((reach, tile, tile), jnp.bfloat16)] * len(slots)
            + out_shape,
            in_specs=[main_memory] * 4 + [vectors, pl.BlockSpec(memory_space=pl.ANY)][: len(more)],
            out_specs=[vectors] * (len(slots) + len(out_shape)),
            scratch_shapes=[
                pltpu.VMEM((len(slots), reach, tile, tile), jnp.bfloat16),
                pltpu.VMEM((tiles, tile, tile), jnp.bfloat16),
                pltpu.SMEM((tiles,), jnp.int32),
                pltpu.SMEM((reach, 1, tiles), jnp.int32),
                pltpu.SMEM((tiles,), jnp.int32),
                pltpu.SemaphoreType.DMA((3 + len(slots),)),
            ],
            compiler_params=FAST,
            name=name,
        )(*inputs, *more)

    head = min(HEAD, aux - 1)
    early = half_rows(list(range(head)), [], [], "half_early")
    *late, own, mixer = half_rows(
        list(range(head, aux - 1)) + [None],
        [metric, early[0]],
        [jax.ShapeDtypeStruct((aux * GROUP, aux * GROUP), jnp.bfloat16)],
        "half_late",
    )
    orders = exchange_orders(aux)
    windows = WINDOWS if len(WINDOWS) == aux - 1 else [4] * aux
    moved = []
    for t, piece in enumerate([*early, *late]):
        if t >= windows[t]:
            piece, _ = lax.optimization_barrier((piece, moved[t - windows[t]]))
        pairs = [
            (2 * i + core, 2 * (i ^ orders[core][t]) + core) for i in range(aux) for core in (0, 1)
        ]
        moved.append(lax.ppermute(piece, ("aux", "bas"), pairs))
    pieces = [own] + moved
    coded = pl.pallas_call(
        gram_kernel,
        out_shape=jax.ShapeDtypeStruct((aux, (reach * reach + 1) * ROWS, tile), jnp.int16),
        in_specs=[vectors] * (aux + 1),
        out_specs=vectors,
        scratch_shapes=[
            pltpu.VMEM((reach * tile, aux * tile), jnp.bfloat16),
        ],
        compiler_params=FAST,
        name="fit_and_gram",
    )(mixer, *pieces)
    received = lax.all_to_all(coded, "aux", split_axis=0, concat_axis=0, tiled=True)
    edge = jnp.where(lax.axis_index("bas") == 0, tiles - 1, 0)
    edge_tile = lax.dynamic_slice_in_dim(received, edge, 1, 0)
    rim = lax.ppermute(edge_tile, "bas", [(0, 1), (1, 0)])
    share = jax.ShapeDtypeStruct((2 * reach - 1, tiles, tile * tile // aux), jnp.float32)
    part = pl.pallas_call(
        functools.partial(band_kernel, reach),
        out_shape=share,
        in_specs=[vectors],
        out_specs=vectors,
        compiler_params=FAST,
        name="band_sum",
    )(received)
    band = pl.pallas_call(
        functools.partial(rim_kernel, reach),
        out_shape=share,
        in_specs=[vectors, vectors],
        out_specs=vectors,
        compiler_params=FAST,
        name="band_rim",
    )(part, rim)
    return jnp.transpose(band, (1, 0, 2))


def solution(mesh):
    placed = (
        P("aux", "bas", None, None, None),
        P("bas", None, None),
        P("bas"),
        P("aux", "bas", None),
        P(),
    )
    return jax.shard_map(
        body, mesh=mesh, in_specs=placed, out_specs=P("bas", None, "aux"), check_vma=False
    )
```

```python
import functools

import jax
import jax.numpy as jnp
from jax import lax
from jax.experimental import pallas as pl
from jax.experimental.pallas import tpu as pltpu
from jax.sharding import PartitionSpec as P

ROWS = 8
LEVELS = 32000.0
GROUP = 16
HEAD = 8
ORDERS = (
    [8, 13, 7, 6, 9, 5, 12, 4, 10, 3, 2, 14, 11, 1, 15],
    [10, 5, 11, 7, 15, 6, 8, 14, 12, 1, 3, 9, 2, 4, 13],
)
CENTRAL = [4, 12, 8, 0, 5, 13, 9, 1, 6, 14, 10, 2, 7, 15, 11, 3]
WINDOWS = [4] * 15
PARTS = 2
STEPS = 128.0
FAST = pltpu.CompilerParams(vmem_limit_bytes=48 * 1024 * 1024)


def exchange_orders(devices):
    if devices - 1 == len(ORDERS[0]):
        return ORDERS
    half = devices // 2
    order = [half]
    for k in range(1, half):
        order += [k, half + k]
    return order, order


def transpose_order(devices):
    if devices == len(CENTRAL):
        return CENTRAL
    return list(range(devices // 2, devices)) + list(range(devices // 2))


def partner(t):
    first, second = exchange_orders(lax.axis_size("aux"))
    return jnp.where(lax.axis_index("bas") == 0, first[t], second[t])


def half_kernel(slots, locality, screen, integrals, orbitals, *rest):
    *halves, taken, factors, places, flags, owner, sems = rest
    if slots[-1] is None:
        metric, _, *halves, mixer = halves
    count, reach, tile, _ = taken.shape
    tiles = factors.shape[0]
    me = lax.axis_index("aux")
    order = [me if t is None else me ^ partner(t) for t in slots]
    total = tiles * lax.axis_size("bas")
    first = lax.axis_index("bas") * tiles
    part = max(count // PARTS, 1)
    small = [
        pltpu.make_async_copy(locality, places, sems.at[0]),
        pltpu.make_async_copy(screen, flags, sems.at[1]),
        pltpu.make_async_copy(orbitals, factors, sems.at[2]),
    ]
    blocks = [
        pltpu.make_async_copy(integrals.at[0, centre], taken.at[k], sems.at[3 + k])
        for k, centre in enumerate(order)
    ]
    for copy in small + blocks:
        copy.start()
    small[0].wait()
    for j in range(tiles):
        owner[places[j]] = j
    small[1].wait()
    small[2].wait()
    if slots[-1] is None:
        write_mixer(metric, mixer)
    for k, centre in enumerate(order):
        if k % part == 0:
            for copy in blocks[k : k + part]:
                copy.wait()
        j = owner[centre]
        product = jnp.dot(
            taken[k].reshape(reach * tile, tile), factors[j], preferred_element_type=jnp.float32
        )
        for d in range(reach):
            block = first + centre + d - reach // 2
            inside = (block >= 0) & (block < total)
            keep = jnp.where(inside, flags[d, 0, j], 0).astype(jnp.float32)
            kept = (product[d * tile : (d + 1) * tile] * keep).astype(jnp.bfloat16)
            halves[k][d] = kept


def write_mixer(metric, mixer):
    aux = metric.shape[0]
    wide = mixer.shape[0]
    group = wide // aux
    me = lax.axis_index("aux")
    slot = lax.broadcasted_iota(jnp.int32, (aux, aux), 0)
    came = jnp.full((aux, aux), me, jnp.int32)
    for t in range(aux - 1):
        came = jnp.where(slot == t + 1, me ^ partner(t), came)
    from_slot = (came == lax.broadcasted_iota(jnp.int32, (aux, aux), 1)).astype(jnp.bfloat16)
    placed = lax.dot_general(
        metric[...], from_slot, (((1,), (1,)), ((), ())), preferred_element_type=jnp.float32
    ).astype(jnp.bfloat16)
    spread = (
        lax.broadcasted_iota(jnp.int32, (wide, aux), 0) // group
        == lax.broadcasted_iota(jnp.int32, (wide, aux), 1)
    ).astype(jnp.bfloat16)
    picked = jnp.dot(spread, placed, preferred_element_type=jnp.float32).astype(jnp.bfloat16)
    full = lax.dot_general(
        picked, spread, (((1,), (1,)), ((), ())), preferred_element_type=jnp.float32
    )
    same_row = (
        lax.broadcasted_iota(jnp.int32, (wide, wide), 0) % group
        == lax.broadcasted_iota(jnp.int32, (wide, wide), 1) % group
    )
    mixer[...] = jnp.where(same_row, full, 0.0).astype(jnp.bfloat16)


def gram_kernel(mixer, *rest):
    *pieces, coded, fitted = rest
    aux = len(pieces)
    reach, tile, _ = pieces[0].shape
    group = GROUP
    wide = aux * group
    for d in range(reach):
        for g in range(0, tile, 2 * group):
            pair = []
            for start in (g, g + group):
                here = slice(start, start + group)
                pair.append(jnp.concatenate([piece[d, here, :] for piece in pieces], axis=0))
            mixed = jnp.dot(
                mixer[...], jnp.concatenate(pair, axis=1), preferred_element_type=jnp.float32
            ).astype(jnp.bfloat16)
            for s in range(2):
                start = d * tile + g + s * group
                for q in range(aux):
                    fitted[start : start + group, q * tile : (q + 1) * tile] = mixed[
                        q * group : (q + 1) * group, s * tile : (s + 1) * tile
                    ]
    gram = lax.dot_general(
        fitted[...], fitted[...], (((1,), (1,)), ((), ())), preferred_element_type=jnp.float32
    )
    lane = lax.broadcasted_iota(jnp.int32, (ROWS, tile), 1)
    owners = coded.shape[0]
    per = tile // owners
    for slot, a in enumerate(transpose_order(owners)):
        codes, scales = [], jnp.zeros((ROWS, tile), jnp.float32)
        for d in range(reach):
            rows = gram[d * tile + a * per : d * tile + (a + 1) * per]
            if per < ROWS:
                rows = jnp.pad(rows, ((0, ROWS - per), (0, 0)))
            code, scale = encode(rows)
            codes += [code[:, d2 * tile : (d2 + 1) * tile] for d2 in range(reach)]
            scales = jnp.where(lane == d, scale, scales)
        sent = jnp.concatenate(codes + [scales], axis=0)
        coded[slot] = sent.astype(jnp.int32).astype(jnp.int16)


def encode(rows):
    peak = jnp.max(jnp.abs(rows), axis=1, keepdims=True)
    scale = jnp.ceil(jnp.log2(jnp.maximum(peak, 1e-37)) * STEPS)
    return jnp.round(rows * jnp.exp2(scale * (-1.0 / STEPS)) * LEVELS), scale


def decode(sent, reach):
    sent = sent.astype(jnp.int32).astype(jnp.float32)
    scales = sent[reach * reach * ROWS :]
    blocks = []
    for d in range(reach):
        factor = jnp.exp2(scales[:, d : d + 1] * (1.0 / STEPS))
        starts = [(d * reach + d2) * ROWS for d2 in range(reach)]
        blocks.append([sent[i : i + ROWS] * (1.0 / LEVELS) * factor for i in starts])
    return blocks


def band_kernel(reach, received, band):
    centres, _, tile = received.shape
    per = band.shape[2] // tile
    offsets = 2 * reach - 1
    middle = reach // 2
    sums = {}

    def finish(m):
        for e in range(offsets):
            total = sums.pop((m, e), jnp.zeros((ROWS, tile), jnp.float32))
            for r in range(per):
                band[e, m : m + 1, r * tile : (r + 1) * tile] = total[r : r + 1]

    order = transpose_order(centres)
    for c in range(centres):
        blocks = decode(received[order.index(c)], reach)
        for d in range(reach):
            m = c + d - middle
            if 0 <= m < centres:
                for d2 in range(reach):
                    key = m, d2 - d + reach - 1
                    piece = blocks[d][d2]
                    sums[key] = sums[key] + piece if key in sums else piece
        if c >= middle:
            finish(c - middle)
    for m in range(centres - middle, centres):
        finish(m)


def rim_kernel(reach, part, rim, band):
    band[...] = part[...]
    tile = rim.shape[2]
    per = band.shape[2] // tile
    blocks = decode(rim[0], reach)

    def add(m, d, first):
        for d2 in range(reach):
            for r in range(per):
                here = first + d2, slice(m, m + 1), slice(r * tile, (r + 1) * tile)
                band[here] += blocks[d][d2][r : r + 1]

    @pl.when(lax.axis_index("bas") == 0)
    def _():
        add(band.shape[1] - 1, 0, reach - 1)

    @pl.when(lax.axis_index("bas") != 0)
    def _():
        add(0, reach - 1, 0)


def body(integrals, orbitals, locality, screen, metric):
    _, tiles, reach, tile, _ = integrals.shape
    aux = lax.axis_size("aux")
    if lax.axis_size("bas") != 2 or tiles != aux or aux & (aux - 1) or reach != 3:
        raise ValueError("unsupported sizes")
    main_memory = pl.BlockSpec(memory_space=pltpu.HBM)
    vectors = pl.BlockSpec(memory_space=pltpu.VMEM)
    inputs = [
        pltpu.with_memory_space_constraint(array, pltpu.HBM)
        for array in (locality, jnp.transpose(screen, (2, 0, 1)), integrals, orbitals)
    ]

    def half_rows(slots, more, out_shape, name):
        return pl.pallas_call(
            functools.partial(half_kernel, slots),
            out_shape=[jax.ShapeDtypeStruct((reach, tile, tile), jnp.bfloat16)] * len(slots)
            + out_shape,
            in_specs=[main_memory] * 4 + [vectors, pl.BlockSpec(memory_space=pl.ANY)][: len(more)],
            out_specs=[vectors] * (len(slots) + len(out_shape)),
            scratch_shapes=[
                pltpu.VMEM((len(slots), reach, tile, tile), jnp.bfloat16),
                pltpu.VMEM((tiles, tile, tile), jnp.bfloat16),
                pltpu.SMEM((tiles,), jnp.int32),
                pltpu.SMEM((reach, 1, tiles), jnp.int32),
                pltpu.SMEM((tiles,), jnp.int32),
                pltpu.SemaphoreType.DMA((3 + len(slots),)),
            ],
            compiler_params=FAST,
            name=name,
        )(*inputs, *more)

    head = min(HEAD, aux - 1)
    early = half_rows(list(range(head)), [], [], "half_early")
    *late, own, mixer = half_rows(
        list(range(head, aux - 1)) + [None],
        [metric, early[0]],
        [jax.ShapeDtypeStruct((aux * GROUP, aux * GROUP), jnp.bfloat16)],
        "half_late",
    )
    orders = exchange_orders(aux)
    windows = WINDOWS if len(WINDOWS) == aux - 1 else [4] * aux
    moved = []
    for t, piece in enumerate([*early, *late]):
        if t >= windows[t]:
            piece, _ = lax.optimization_barrier((piece, moved[t - windows[t]]))
        pairs = [
            (2 * i + core, 2 * (i ^ orders[core][t]) + core) for i in range(aux) for core in (0, 1)
        ]
        moved.append(lax.ppermute(piece, ("aux", "bas"), pairs))
    pieces = [own] + moved
    coded = pl.pallas_call(
        gram_kernel,
        out_shape=jax.ShapeDtypeStruct((aux, (reach * reach + 1) * ROWS, tile), jnp.int16),
        in_specs=[vectors] * (aux + 1),
        out_specs=vectors,
        scratch_shapes=[
            pltpu.VMEM((reach * tile, aux * tile), jnp.bfloat16),
        ],
        compiler_params=FAST,
        name="fit_and_gram",
    )(mixer, *pieces)
    order = transpose_order(aux)
    received = lax.all_to_all(
        coded, "aux", split_axis=0, concat_axis=0, tiled=True, axis_index_groups=[order]
    )
    edge = jnp.where(lax.axis_index("bas") == 0, order.index(tiles - 1), order.index(0))
    edge_tile = lax.dynamic_slice_in_dim(received, edge, 1, 0)
    rim = lax.ppermute(edge_tile, "bas", [(0, 1), (1, 0)])
    share = jax.ShapeDtypeStruct((2 * reach - 1, tiles, tile * tile // aux), jnp.float32)
    part = pl.pallas_call(
        functools.partial(band_kernel, reach),
        out_shape=share,
        in_specs=[vectors],
        out_specs=vectors,
        compiler_params=FAST,
        name="band_sum",
    )(received)
    band = pl.pallas_call(
        functools.partial(rim_kernel, reach),
        out_shape=share,
        in_specs=[vectors, vectors],
        out_specs=vectors,
        compiler_params=FAST,
        name="band_rim",
    )(part, rim)
    return jnp.transpose(band, (1, 0, 2))


def solution(mesh):
    placed = (
        P("aux", "bas", None, None, None),
        P("bas", None, None),
        P("bas"),
        P("aux", "bas", None),
        P(),
    )
    return jax.shard_map(
        body, mesh=mesh, in_specs=placed, out_specs=P("bas", None, "aux"), check_vma=False
    )
```
